32 devices in a mesh: rep: 2 (over x), tile: 16 (over z, y, core).
Axes of the slice: x: 2, y: 2, z: 4, core: 2. Of those that a mesh axis runs over, the one named last changes fastest.
Arguments:
- mode_field: bfloat16 [120, 128, 32, 128], P(None, ('rep', 'tile')), parts along dimension 1, may hold values from -6 to 6
- conductivity: bfloat16 [36, 128, 32, 128], P(None, ('rep', 'tile')), parts along dimension 1, may hold values from -6 to 6
- triple_out: int32 [4096], replicated, may hold values from 0 to 119
- triple_in: int32 [4096], replicated, may hold values from 0 to 119
- triple_coef: int32 [4096], replicated, may hold values from 0 to 35
- triple_value: float32 [4096], replicated, may hold values from -1 to 1
Outputs:
- applied: bfloat16 [120, 128, 32, 128], P(None, ('rep', 'tile')), parts along dimension 1
The draws below stay inside these ranges and needn't reach their ends.
There are 2 independent parts, one for each index of `rep`. The reference program is written for one: setup_inputs(seed, part) draws one part's arguments, and reference() takes and returns one part's arrays. A program takes and returns all parts, laid end to end along the dimension named above; an argument that names none is the same for every part. Nothing has to cross between parts.
Inputs may be any that keep to these rules, and one draw needn't show every extreme that they name: triple_out, triple_in and triple_coef at the same position name one coupling; repeated couplings add.
All inputs are finite; a program needn't handle non-finite values.
Results may differ from the reference program's by a relative error of at most 0.0057.
Values may be sent and summed in bfloat16 or wider, within the bound.
A program may use at most 64 MiB of HBM per device.

```python
import jax
import jax.numpy as jnp
from jax import lax

P_SIZE = 120
K = 36
NNZ = 4096
NX = 32
NY = 128
NZ = 64


def place_ends(array, stream_key, least, high):
    spot = [jax.random.randint(jax.random.fold_in(stream_key, axis), (), 0, length) for axis, length in enumerate(array.shape)]
    longest = array.shape.index(max(array.shape))
    neighbour = spot[:longest] + [(spot[longest] + 1) % array.shape[longest]] + spot[longest + 1:]
    return array.at[tuple(spot)].set(least).at[tuple(neighbour)].set(high)


def steps_of(rng, dims, split, low, top_value):
    loudness = 1.0
    for axis_at, parts in split:
        steps = jax.random.uniform(jax.random.fold_in(jax.random.fold_in(rng, 6), axis_at), (parts,), jnp.float32, low / len(split), top_value / len(split))
        loudness = loudness * jnp.repeat(jnp.exp(steps), dims[axis_at] // parts).reshape((-1,) + (1,) * (len(dims) - 1 - axis_at))
    return loudness


def normal_values(stream_key, shape, deviation, bound, shards=(), kind=jnp.bfloat16):
    gain = steps_of(stream_key, shape, shards, -0.22, 0.18) if shards else 1.0
    array = jax.random.normal(stream_key, shape, jnp.float32) * deviation * gain
    return jnp.minimum(jnp.maximum(array, -bound), bound).astype(kind)


def setup_inputs(seed: int = 0, part: int = 0) -> dict:
    arg_keys = jax.random.split(jax.random.key(seed), 7)
    own_keys = jax.random.split(jax.random.fold_in(arg_keys[6], part), 7)
    return {
        "mode_field": normal_values(own_keys[0], (P_SIZE, NZ, NX, NY), 1.0, 6.0, ((1, 16),)),
        "conductivity": normal_values(own_keys[1], (K, NZ, NX, NY), 1.0, 6.0, ((1, 16),)),
        "triple_out": place_ends(jax.random.randint(arg_keys[2], (NNZ,), 0, P_SIZE), jax.random.fold_in(arg_keys[2], 1), 0, P_SIZE - 1).astype(jnp.int32),
        "triple_in": place_ends(jax.random.randint(arg_keys[3], (NNZ,), 0, P_SIZE), jax.random.fold_in(arg_keys[3], 1), 0, P_SIZE - 1).astype(jnp.int32),
        "triple_coef": place_ends(jax.random.randint(arg_keys[4], (NNZ,), 0, K), jax.random.fold_in(arg_keys[4], 1), 0, K - 1).astype(jnp.int32),
        "triple_value": normal_values(arg_keys[5], (NNZ,), 0.07, 1.0, (), jnp.float32),
    }


def coupling_matrix(triple_out, triple_in, triple_coef, triple_value, modes, coefs):
    flat_index = (triple_out * (coefs * modes) + triple_coef * modes + triple_in).astype(jnp.int32)
    dense_terms = jax.ops.segment_sum(triple_value.astype(jnp.float32), flat_index, num_segments=modes * coefs * modes)
    return dense_terms.reshape(modes, coefs * modes).astype(jnp.bfloat16)


def face_terms(mode_block, cond_block):
    center_mode = mode_block[:, 1, 1:-1, 1:-1]
    center_cond = cond_block[:, 1, 1:-1, 1:-1]
    picks = [
        lambda b: b[:, 0, 1:-1, 1:-1],
        lambda b: b[:, 2, 1:-1, 1:-1],
        lambda b: b[:, 1, :-2, 1:-1],
        lambda b: b[:, 1, 2:, 1:-1],
        lambda b: b[:, 1, 1:-1, :-2],
        lambda b: b[:, 1, 1:-1, 2:],
    ]
    total = jnp.zeros((cond_block.shape[0],) + center_mode.shape, jnp.float32)
    for pick in picks:
        face_cond = 0.5 * (center_cond + pick(cond_block))
        total = total + face_cond[:, None] * (center_mode - pick(mode_block))[None]
    return total


def reference(mode_field, conductivity, triple_out, triple_in, triple_coef, triple_value):
    coupling = coupling_matrix(triple_out, triple_in, triple_coef, triple_value, P_SIZE, K)
    mode_pad = jnp.pad(mode_field.astype(jnp.float32), ((0, 0), (1, 1), (1, 1), (1, 1)))
    cond_pad = jnp.pad(conductivity.astype(jnp.float32), ((0, 0), (1, 1), (1, 1), (1, 1)))

    def one_layer(layer_index):
        mode_block = lax.dynamic_slice_in_dim(mode_pad, layer_index, 3, 1)
        cond_block = lax.dynamic_slice_in_dim(cond_pad, layer_index, 3, 1)
        terms_now = face_terms(mode_block, cond_block).astype(jnp.bfloat16)
        result = jnp.dot(coupling, terms_now.reshape(K * P_SIZE, NX * NY), preferred_element_type=jnp.float32)
        return result.astype(jnp.bfloat16).reshape(P_SIZE, NX, NY)

    layers = lax.map(one_layer, jnp.arange(NZ, dtype=jnp.int32))
    return jnp.transpose(layers, (1, 0, 2, 3))
```

```python
import functools
import jax
import jax.numpy as jnp
from jax import lax
from jax.experimental import pallas as pl
from jax.experimental.pallas import tpu as pltpu
from jax.sharding import PartitionSpec as P

LANES = 128
COPIES = 4


def coupling_kernel(coefs, modes, row_ref, in_ref, value_ref, out_ref, *sums):
    for s in sums:
        s[...] = jnp.zeros_like(s)
    lane = lax.broadcasted_iota(jnp.int32, (1, LANES), 1)
    n = row_ref.shape[0]

    def step(t, carry):
        for u in range(4):
            for c in range(COPIES):
                at = t * (4 * COPIES) + u * COPIES + c
                row = row_ref[at]
                hit = jnp.where(lane == in_ref[at], value_ref[at], 0.0)
                sums[c][pl.ds(row, 1), :] += hit
        return carry

    lax.fori_loop(0, n // (4 * COPIES), step, 0)
    for k in range(coefs):
        rows = pl.ds(k * LANES, LANES)
        total = sums[0][rows, :]
        for c in range(1, COPIES):
            total = total + sums[c][rows, :]
        out_ref[:, k * LANES : (k + 1) * LANES] = total[:modes].astype(jnp.bfloat16)


def coupling_matrix(triple_out, triple_in, triple_coef, triple_value, modes, coefs):
    rows = triple_coef * LANES + triple_out
    smem = pl.BlockSpec(memory_space=pltpu.SMEM)
    return pl.pallas_call(
        functools.partial(coupling_kernel, coefs, modes),
        out_shape=jax.ShapeDtypeStruct((modes, coefs * LANES), jnp.bfloat16),
        in_specs=[smem] * 3,
        out_specs=pl.BlockSpec(memory_space=pltpu.VMEM),
        scratch_shapes=[pltpu.VMEM((coefs * LANES, LANES), jnp.float32)] * COPIES,
        cost_estimate=pl.CostEstimate(flops=40_000_000, bytes_accessed=40_000_000, transcendentals=0),
        compiler_params=pltpu.CompilerParams(vmem_limit_bytes=40 << 20),
    )(rows, triple_in, triple_value)


def main_kernel(coefs, modes, depth, rows, c_ref, m_ref, k_ref, o_ref, dm, kf, kb, terms):
    lane = lax.broadcasted_iota(jnp.int32, (1, LANES), 1)

    def shifted(v):
        before = jnp.where(lane == 0, 0.0, pltpu.roll(v, 1, 1))
        after = jnp.where(lane == LANES - 1, 0.0, pltpu.roll(v, LANES - 1, 1))
        return before, after

    def around(ref, z, y):
        f32 = jnp.float32
        center = ref[z, y].astype(f32)
        return center, (
            ref[z - 1, y].astype(f32),
            ref[z + 1, y].astype(f32),
            ref[z, y - 1].astype(f32),
            ref[z, y + 1].astype(f32),
        ) + shifted(center)

    def prepare(z, y, r):
        center, near = around(m_ref, z, y)
        for d in range(6):
            dm[r, d] = (center - near[d]).astype(jnp.bfloat16)
        center, near = around(k_ref, z, y)
        for d in range(6):
            kf[r, d] = 0.5 * (center + near[d])
        for d in range(6):
            for k in range(coefs):
                row = jnp.broadcast_to(kf[r, d, k : k + 1, :], (16, LANES))
                kb[r, d, k] = row.astype(jnp.bfloat16)

    def fill(slot):
        for r in range(2):
            for jg in range(LANES // 64):
                parts = [[dm[r, d, jg * 64 + 16 * q : jg * 64 + 16 * q + 16, :] for q in range(4)] for d in range(6)]
                for k in range(coefs):
                    face = [kb[r, d, k] for d in range(6)]
                    for q in range(4):
                        p = [face[d] * parts[d][q] for d in range(6)]
                        t = (p[0] + p[1]) + (p[2] + p[3]) + (p[4] + p[5])
                        at = k * LANES + jg * 64 + 16 * q
                        terms[slot, at : at + 16, r * LANES : (r + 1) * LANES] = t

    def place(s):
        pairs = rows // 2
        return s // pairs + 1, s % pairs * 2 + 1

    def multiply(s, slot):
        z, y = place(s)
        got = jnp.dot(c_ref[...], terms[slot], preferred_element_type=jnp.float32)
        for r in range(2):
            o_ref[z - 1, y - 1 + r] = got[:, r * LANES : (r + 1) * LANES].astype(jnp.bfloat16)

    def ready(s, slot):
        z, y = place(s)
        for r in range(2):
            prepare(z, y + r, r)
        fill(slot)

    total = depth * rows // 2
    ready(0, 0)

    def step(h, carry):
        s = h * 2
        ready(s + 1, 1)
        multiply(s, 0)
        ready(jnp.minimum(s + 2, total - 1), 0)
        multiply(s + 1, 1)
        return carry

    lax.fori_loop(0, total // 2, step, 0)


def per_device(mode_field, conductivity, triple_out, triple_in, triple_coef, triple_value):
    modes, depth, rows, lanes = mode_field.shape
    coefs = conductivity.shape[0]
    coefs_pad = -(-coefs // 16) * 16
    coupling = coupling_matrix(triple_out, triple_in, triple_coef, triple_value, modes, coefs)
    devices = lax.axis_size("tile")
    up = [(i, i + 1) for i in range(devices - 1)]
    down = [(j, i) for i, j in up]

    def extend(shard, pad):
        before = lax.ppermute(shard[:, -1:], "tile", up)
        after = lax.ppermute(shard[:, :1], "tile", down)
        whole = jnp.concatenate([before, shard, after], axis=1)
        whole = jnp.transpose(whole, (1, 2, 0, 3))
        return jnp.pad(whole, ((0, 0), (1, 1), (0, pad), (0, 0)))

    m_ext = extend(mode_field, LANES - modes)
    k_ext = extend(conductivity, coefs_pad - coefs)
    vmem = pl.BlockSpec(memory_space=pltpu.VMEM)
    out = pl.pallas_call(
        functools.partial(main_kernel, coefs, modes, depth, rows),
        out_shape=jax.ShapeDtypeStruct((depth, rows, modes, lanes), jnp.bfloat16),
        in_specs=[vmem] * 3,
        out_specs=vmem,
        scratch_shapes=[
            pltpu.VMEM((2, 6, LANES, LANES), jnp.bfloat16),
            pltpu.VMEM((2, 6, coefs_pad, LANES), jnp.float32),
            pltpu.VMEM((2, 6, coefs, 16, LANES), jnp.bfloat16),
            pltpu.VMEM((2, coefs * LANES, 2 * LANES), jnp.bfloat16),
        ],
        compiler_params=pltpu.CompilerParams(vmem_limit_bytes=48 << 20),
    )(coupling, m_ext, k_ext)
    return jnp.transpose(out, (2, 0, 1, 3))


def solution(mesh):
    return jax.shard_map(
        per_device,
        mesh=mesh,
        in_specs=(
            P(None, ("rep", "tile"), None, None),
            P(None, ("rep", "tile"), None, None),
            P(),
            P(),
            P(),
            P(),
        ),
        out_specs=P(None, ("rep", "tile"), None, None),
        check_vma=False,
    )
```

```python
import functools
import jax
import jax.numpy as jnp
from jax import lax
from jax.experimental import pallas as pl
from jax.experimental.pallas import tpu as pltpu
from jax.sharding import PartitionSpec as P

LANES = 128
COPIES = 4
GROUP = 6


def coupling_kernel(coefs, modes, row_ref, in_ref, value_ref, out_ref, *sums):
    for s in sums:
        s[...] = jnp.zeros_like(s)
    lane = lax.broadcasted_iota(jnp.int32, (1, LANES), 1)
    n = row_ref.shape[0]

    def step(t, carry):
        for u in range(4):
            for c in range(COPIES):
                at = t * (4 * COPIES) + u * COPIES + c
                row = row_ref[at]
                hit = jnp.where(lane == in_ref[at], value_ref[at], 0.0)
                sums[c][pl.ds(row, 1), :] += hit
        return carry

    lax.fori_loop(0, n // (4 * COPIES), step, 0)
    for k in range(coefs):
        rows = pl.ds(k * LANES, LANES)
        total = sums[0][rows, :]
        for c in range(1, COPIES):
            total = total + sums[c][rows, :]
        out_ref[:, k * LANES : (k + 1) * LANES] = total[:modes].astype(jnp.bfloat16)


def coupling_matrix(triple_out, triple_in, triple_coef, triple_value, modes, coefs):
    rows = triple_coef * LANES + triple_out
    smem = pl.BlockSpec(memory_space=pltpu.SMEM)
    return pl.pallas_call(
        functools.partial(coupling_kernel, coefs, modes),
        out_shape=jax.ShapeDtypeStruct((modes, coefs * LANES), jnp.bfloat16),
        in_specs=[smem] * 3,
        out_specs=pl.BlockSpec(memory_space=pltpu.VMEM),
        scratch_shapes=[pltpu.VMEM((coefs * LANES, LANES), jnp.float32)] * COPIES,
        cost_estimate=pl.CostEstimate(flops=40_000_000, bytes_accessed=40_000_000, transcendentals=0),
        compiler_params=pltpu.CompilerParams(vmem_limit_bytes=40 << 20),
    )(rows, triple_in, triple_value)


def main_kernel(coefs, modes, depth, rows, c_ref, m_ref, k_ref, o_ref, dm, kf, kb, terms):
    lane = lax.broadcasted_iota(jnp.int32, (1, LANES), 1)

    def shifted(v):
        before = jnp.where(lane == 0, 0.0, pltpu.roll(v, 1, 1))
        after = jnp.where(lane == LANES - 1, 0.0, pltpu.roll(v, LANES - 1, 1))
        return before, after

    def around(ref, z, y):
        f32 = jnp.float32
        center = ref[z, y].astype(f32)
        return center, (
            ref[z - 1, y].astype(f32),
            ref[z + 1, y].astype(f32),
            ref[z, y - 1].astype(f32),
            ref[z, y + 1].astype(f32),
        ) + shifted(center)

    def prepare(z, y, r):
        center, near = around(m_ref, z, y)
        for d in range(6):
            dm[r, d] = (center - near[d]).astype(jnp.bfloat16)
        center, near = around(k_ref, z, y)
        for d in range(6):
            kf[r, d] = 0.5 * (center + near[d])
        for d in range(6):
            for k in range(coefs):
                row = jnp.broadcast_to(kf[r, d, k : k + 1, :], (16, LANES))
                kb[r, d, k] = row.astype(jnp.bfloat16)

    def fill(slot, g):
        base = pl.multiple_of(g * (GROUP * LANES), GROUP * LANES)
        for r in range(2):
            for jg in range(LANES // 64):
                parts = [[dm[r, d, jg * 64 + 16 * q : jg * 64 + 16 * q + 16, :] for q in range(4)] for d in range(6)]
                for k in range(GROUP):
                    face = [kb[r, d, g * GROUP + k] for d in range(6)]
                    for q in range(4):
                        p = [face[d] * parts[d][q] for d in range(6)]
                        t = (p[0] + p[1]) + (p[2] + p[3]) + (p[4] + p[5])
                        at = k * LANES + jg * 64 + 16 * q
                        terms[slot, pl.ds(base + at, 16), r * LANES : (r + 1) * LANES] = t

    def place(s):
        pairs = rows // 2
        return s // pairs + 1, s % pairs * 2 + 1

    total = depth * rows // 2

    def ready(s):
        z, y = place(s)
        for r in range(2):
            prepare(z, y + r, r)

    def store(s, got):
        z, y = place(s)
        for r in range(2):
            o_ref[z - 1, y - 1 + r] = got[:, r * LANES : (r + 1) * LANES].astype(jnp.bfloat16)

    def step(s, carry):
        ready(s)

        def group(g, inner):
            fill(0, g)
            return inner

        lax.fori_loop(0, coefs // GROUP, group, 0)
        store(s, jnp.dot(c_ref[...], terms[0], preferred_element_type=jnp.float32))
        return carry

    lax.fori_loop(0, total, step, 0)


def per_device(mode_field, conductivity, triple_out, triple_in, triple_coef, triple_value):
    modes, depth, rows, lanes = mode_field.shape
    coefs = conductivity.shape[0]
    coefs_pad = -(-coefs // 16) * 16
    coupling = coupling_matrix(triple_out, triple_in, triple_coef, triple_value, modes, coefs)
    devices = lax.axis_size("tile")
    up = [(i, i + 1) for i in range(devices - 1)]
    down = [(j, i) for i, j in up]

    def extend(shard, pad):
        before = lax.ppermute(shard[:, -1:], "tile", up)
        after = lax.ppermute(shard[:, :1], "tile", down)
        whole = jnp.concatenate([before, shard, after], axis=1)
        whole = jnp.transpose(whole, (1, 2, 0, 3))
        return jnp.pad(whole, ((0, 0), (1, 1), (0, pad), (0, 0)))

    m_ext = extend(mode_field, LANES - modes)
    k_ext = extend(conductivity, coefs_pad - coefs)
    vmem = pl.BlockSpec(memory_space=pltpu.VMEM)
    out = pl.pallas_call(
        functools.partial(main_kernel, coefs, modes, depth, rows),
        out_shape=jax.ShapeDtypeStruct((depth, rows, modes, lanes), jnp.bfloat16),
        in_specs=[vmem] * 3,
        out_specs=vmem,
        scratch_shapes=[
            pltpu.VMEM((2, 6, LANES, LANES), jnp.bfloat16),
            pltpu.VMEM((2, 6, coefs_pad, LANES), jnp.float32),
            pltpu.VMEM((2, 6, coefs, 16, LANES), jnp.bfloat16),
            pltpu.VMEM((1, coefs * LANES, 2 * LANES), jnp.bfloat16),
        ],
        compiler_params=pltpu.CompilerParams(vmem_limit_bytes=48 << 20),
    )(coupling, m_ext, k_ext)
    return jnp.transpose(out, (2, 0, 1, 3))


def solution(mesh):
    return jax.shard_map(
        per_device,
        mesh=mesh,
        in_specs=(
            P(None, ("rep", "tile"), None, None),
            P(None, ("rep", "tile"), None, None),
            P(),
            P(),
            P(),
            P(),
        ),
        out_specs=P(None, ("rep", "tile"), None, None),
        check_vma=False,
    )
```

```python
import functools
import jax
import jax.numpy as jnp
from jax import lax
from jax.experimental import pallas as pl
from jax.experimental.pallas import tpu as pltpu
from jax.sharding import PartitionSpec as P

LANES = 128
COPIES = 4
GROUP = 6


def coupling_kernel(coefs, modes, row_ref, in_ref, value_ref, out_ref, *sums):
    for s in sums:
        s[...] = jnp.zeros_like(s)
    lane = lax.broadcasted_iota(jnp.int32, (1, LANES), 1)
    n = row_ref.shape[0]

    def step(t, carry):
        for u in range(4):
            for c in range(COPIES):
                at = t * (4 * COPIES) + u * COPIES + c
                row = row_ref[at]
                hit = jnp.where(lane == in_ref[at], value_ref[at], 0.0)
                sums[c][pl.ds(row, 1), :] += hit
        return carry

    lax.fori_loop(0, n // (4 * COPIES), step, 0)
    for k in range(coefs):
        rows = pl.ds(k * LANES, LANES)
        total = sums[0][rows, :]
        for c in range(1, COPIES):
            total = total + sums[c][rows, :]
        out_ref[:, k * LANES : (k + 1) * LANES] = total[:modes].astype(jnp.bfloat16)


def coupling_matrix(triple_out, triple_in, triple_coef, triple_value, modes, coefs):
    rows = triple_coef * LANES + triple_out
    smem = pl.BlockSpec(memory_space=pltpu.SMEM)
    return pl.pallas_call(
        functools.partial(coupling_kernel, coefs, modes),
        out_shape=jax.ShapeDtypeStruct((modes, coefs * LANES), jnp.bfloat16),
        in_specs=[smem] * 3,
        out_specs=pl.BlockSpec(memory_space=pltpu.VMEM),
        scratch_shapes=[pltpu.VMEM((coefs * LANES, LANES), jnp.float32)] * COPIES,
        cost_estimate=pl.CostEstimate(flops=40_000_000, bytes_accessed=40_000_000, transcendentals=0),
        compiler_params=pltpu.CompilerParams(vmem_limit_bytes=40 << 20),
    )(rows, triple_in, triple_value)


def assemble(ref, whole, before, after, depth, rows):
    pad = ref.shape[2] - whole.shape[2]
    blank = jnp.zeros(ref.shape[2:], ref.dtype)
    for z in range(depth + 2):
        ref[z, 0] = blank
        ref[z, rows + 1] = blank

    def widen(v):
        edge = jnp.zeros((pad, v.shape[1]), jnp.float32)
        return jnp.concatenate([v.astype(jnp.float32), edge], axis=0).astype(ref.dtype)

    def row(y, carry):
        ref[0, y + 1] = widen(before[0, y])
        ref[depth + 1, y + 1] = widen(after[0, y])
        for z in range(depth):
            ref[z + 1, y + 1] = widen(whole[z, y])
        return carry

    lax.fori_loop(0, rows, row, 0)


def main_kernel(coefs, modes, depth, rows, c_ref, m_in, m_before, m_after, k_in, k_before, k_after, o_ref, m_ref, k_ref, dm, kf, kb, terms):
    for ref, whole, before, after in ((m_ref, m_in, m_before, m_after), (k_ref, k_in, k_before, k_after)):
        assemble(ref, whole, before, after, depth, rows)

    lane = lax.broadcasted_iota(jnp.int32, (1, LANES), 1)

    def shifted(v):
        before = jnp.where(lane == 0, 0.0, pltpu.roll(v, 1, 1))
        after = jnp.where(lane == LANES - 1, 0.0, pltpu.roll(v, LANES - 1, 1))
        return before, after

    def around(ref, z, y):
        f32 = jnp.float32
        center = ref[z, y].astype(f32)
        return center, (
            ref[z - 1, y].astype(f32),
            ref[z + 1, y].astype(f32),
            ref[z, y - 1].astype(f32),
            ref[z, y + 1].astype(f32),
        ) + shifted(center)

    def prepare(z, y, r):
        center, near = around(m_ref, z, y)
        for d in range(6):
            dm[r, d] = (center - near[d]).astype(jnp.bfloat16)
        center, near = around(k_ref, z, y)
        for d in range(6):
            kf[r, d] = 0.5 * (center + near[d])
        for d in range(6):
            for k in range(coefs):
                row = jnp.broadcast_to(kf[r, d, k : k + 1, :], (16, LANES))
                kb[r, d, k] = row.astype(jnp.bfloat16)

    def fill(slot, g):
        base = pl.multiple_of(g * (GROUP * LANES), GROUP * LANES)
        for r in range(2):
            for jg in range(LANES // 64):
                parts = [[dm[r, d, jg * 64 + 16 * q : jg * 64 + 16 * q + 16, :] for q in range(4)] for d in range(6)]
                for k in range(GROUP):
                    face = [kb[r, d, g * GROUP + k] for d in range(6)]
                    for q in range(4):
                        p = [face[d] * parts[d][q] for d in range(6)]
                        t = (p[0] + p[1]) + (p[2] + p[3]) + (p[4] + p[5])
                        at = k * LANES + jg * 64 + 16 * q
                        terms[slot, pl.ds(base + at, 16), r * LANES : (r + 1) * LANES] = t

    def place(s):
        pairs = rows // 2
        return s // pairs + 1, s % pairs * 2 + 1

    total = depth * rows // 2

    def ready(s):
        z, y = place(s)
        for r in range(2):
            prepare(z, y + r, r)

    def store(s, got):
        z, y = place(s)
        for r in range(2):
            o_ref[z - 1, y - 1 + r] = got[:, r * LANES : (r + 1) * LANES].astype(jnp.bfloat16)

    def step(s, carry):
        ready(s)

        def group(g, inner):
            fill(0, g)
            return inner

        lax.fori_loop(0, coefs // GROUP, group, 0)
        store(s, jnp.dot(c_ref[...], terms[0], preferred_element_type=jnp.float32))
        return carry

    lax.fori_loop(0, total, step, 0)


def per_device(mode_field, conductivity, triple_out, triple_in, triple_coef, triple_value):
    modes, depth, rows, lanes = mode_field.shape
    coefs = conductivity.shape[0]
    coefs_pad = -(-coefs // 16) * 16
    coupling = coupling_matrix(triple_out, triple_in, triple_coef, triple_value, modes, coefs)
    devices = lax.axis_size("tile")
    up = [(i, i + 1) for i in range(devices - 1)]
    down = [(j, i) for i, j in up]

    def extend(shard):
        before = lax.ppermute(shard[:, -1:], "tile", up)
        after = lax.ppermute(shard[:, :1], "tile", down)
        return [jnp.transpose(part, (1, 2, 0, 3)) for part in (shard, before, after)]

    m_parts = extend(mode_field)
    k_parts = extend(conductivity)
    vmem = pl.BlockSpec(memory_space=pltpu.VMEM)
    out = pl.pallas_call(
        functools.partial(main_kernel, coefs, modes, depth, rows),
        out_shape=jax.ShapeDtypeStruct((depth, rows, modes, lanes), jnp.bfloat16),
        in_specs=[vmem] * 7,
        out_specs=vmem,
        scratch_shapes=[
            pltpu.VMEM((depth + 2, rows + 2, LANES, lanes), jnp.bfloat16),
            pltpu.VMEM((depth + 2, rows + 2, coefs_pad, lanes), jnp.bfloat16),
            pltpu.VMEM((2, 6, LANES, LANES), jnp.bfloat16),
            pltpu.VMEM((2, 6, coefs_pad, LANES), jnp.float32),
            pltpu.VMEM((2, 6, coefs, 16, LANES), jnp.bfloat16),
            pltpu.VMEM((1, coefs * LANES, 2 * LANES), jnp.bfloat16),
        ],
        compiler_params=pltpu.CompilerParams(vmem_limit_bytes=48 << 20),
    )(coupling, *m_parts, *k_parts)
    return jnp.transpose(out, (2, 0, 1, 3))


def solution(mesh):
    return jax.shard_map(
        per_device,
        mesh=mesh,
        in_specs=(
            P(None, ("rep", "tile"), None, None),
            P(None, ("rep", "tile"), None, None),
            P(),
            P(),
            P(),
            P(),
        ),
        out_specs=P(None, ("rep", "tile"), None, None),
        check_vma=False,
    )
```

```python
import functools
import jax
import jax.numpy as jnp
from jax import lax
from jax.experimental import pallas as pl
from jax.experimental.pallas import tpu as pltpu
from jax.sharding import PartitionSpec as P

LANES = 128
COPIES = 4
GROUP = 12


def coupling_kernel(coefs, modes, row_ref, in_ref, value_ref, out_ref, *sums):
    for s in sums:
        s[...] = jnp.zeros_like(s)
    lane = lax.broadcasted_iota(jnp.int32, (1, LANES), 1)
    n = row_ref.shape[0]

    def step(t, carry):
        for u in range(4):
            for c in range(COPIES):
                at = t * (4 * COPIES) + u * COPIES + c
                row = row_ref[at]
                hit = jnp.where(lane == in_ref[at], value_ref[at], 0.0)
                sums[c][pl.ds(row, 1), :] += hit
        return carry

    lax.fori_loop(0, n // (4 * COPIES), step, 0)
    for k in range(coefs):
        rows = pl.ds(k * LANES, LANES)
        total = sums[0][rows, :]
        for c in range(1, COPIES):
            total = total + sums[c][rows, :]
        out_ref[:, k * LANES : (k + 1) * LANES] = total[:modes].astype(jnp.bfloat16)


def coupling_matrix(triple_out, triple_in, triple_coef, triple_value, modes, coefs):
    rows = triple_coef * LANES + triple_out
    smem = pl.BlockSpec(memory_space=pltpu.SMEM)
    return pl.pallas_call(
        functools.partial(coupling_kernel, coefs, modes),
        out_shape=jax.ShapeDtypeStruct((modes, coefs * LANES), jnp.bfloat16),
        in_specs=[smem] * 3,
        out_specs=pl.BlockSpec(memory_space=pltpu.VMEM),
        scratch_shapes=[pltpu.VMEM((coefs * LANES, LANES), jnp.float32)] * COPIES,
        cost_estimate=pl.CostEstimate(flops=40_000_000, bytes_accessed=40_000_000, transcendentals=0),
        compiler_params=pltpu.CompilerParams(vmem_limit_bytes=40 << 20),
    )(rows, triple_in, triple_value)


def assemble(ref, whole, before, after, depth, rows):
    pad = ref.shape[2] - whole.shape[2]
    blank = jnp.zeros(ref.shape[2:], ref.dtype)
    for z in range(depth + 2):
        ref[z, 0] = blank
        ref[z, rows + 1] = blank

    def widen(v):
        edge = jnp.zeros((pad, v.shape[1]), jnp.float32)
        return jnp.concatenate([v.astype(jnp.float32), edge], axis=0).astype(ref.dtype)

    def row(y, carry):
        ref[0, y + 1] = widen(before[0, y])
        ref[depth + 1, y + 1] = widen(after[0, y])
        for z in range(depth):
            ref[z + 1, y + 1] = widen(whole[z, y])
        return carry

    lax.fori_loop(0, rows, row, 0)


def main_kernel(coefs, modes, depth, rows, c_ref, m_in, m_before, m_after, k_in, k_before, k_after, o_ref, m_ref, k_ref, dm, kf, kb, terms):
    for ref, whole, before, after in ((m_ref, m_in, m_before, m_after), (k_ref, k_in, k_before, k_after)):
        assemble(ref, whole, before, after, depth, rows)

    lane = lax.broadcasted_iota(jnp.int32, (1, LANES), 1)

    def shifted(v):
        before = jnp.where(lane == 0, 0.0, pltpu.roll(v, 1, 1))
        after = jnp.where(lane == LANES - 1, 0.0, pltpu.roll(v, LANES - 1, 1))
        return before, after

    def around(ref, z, y):
        f32 = jnp.float32
        center = ref[z, y].astype(f32)
        return center, (
            ref[z - 1, y].astype(f32),
            ref[z + 1, y].astype(f32),
            ref[z, y - 1].astype(f32),
            ref[z, y + 1].astype(f32),
        ) + shifted(center)

    def prepare(z, y, r):
        center, near = around(m_ref, z, y)
        for d in range(6):
            dm[r, d] = (center - near[d]).astype(jnp.bfloat16)
        center, near = around(k_ref, z, y)
        for d in range(6):
            kf[r, d] = 0.5 * (center + near[d])
        for d in range(6):
            for k in range(coefs):
                row = jnp.broadcast_to(kf[r, d, k : k + 1, :], (16, LANES))
                kb[r, d, k] = row.astype(jnp.bfloat16)

    def fill(slot, g):
        base = pl.multiple_of(g * (GROUP * LANES), GROUP * LANES)
        for r in range(2):
            for jg in range(LANES // 64):
                parts = [[dm[r, d, jg * 64 + 16 * q : jg * 64 + 16 * q + 16, :] for q in range(4)] for d in range(6)]
                for k in range(GROUP):
                    face = [kb[r, d, g * GROUP + k] for d in range(6)]
                    for q in range(4):
                        p = [face[d] * parts[d][q] for d in range(6)]
                        t = (p[0] + p[1]) + (p[2] + p[3]) + (p[4] + p[5])
                        at = k * LANES + jg * 64 + 16 * q
                        terms[slot, pl.ds(base + at, 16), r * LANES : (r + 1) * LANES] = t

    def place(s):
        pairs = rows // 2
        return s // pairs + 1, s % pairs * 2 + 1

    total = depth * rows // 2

    def ready(s):
        z, y = place(s)
        for r in range(2):
            prepare(z, y + r, r)

    def store(s, got):
        z, y = place(s)
        for r in range(2):
            o_ref[z - 1, y - 1 + r] = got[:, r * LANES : (r + 1) * LANES].astype(jnp.bfloat16)

    def step(s, carry):
        ready(s)

        def group(g, inner):
            fill(0, g)
            return inner

        lax.fori_loop(0, coefs // GROUP, group, 0)
        store(s, jnp.dot(c_ref[...], terms[0], preferred_element_type=jnp.float32))
        return carry

    lax.fori_loop(0, total, step, 0)


def per_device(mode_field, conductivity, triple_out, triple_in, triple_coef, triple_value):
    modes, depth, rows, lanes = mode_field.shape
    coefs = conductivity.shape[0]
    coefs_pad = -(-coefs // 16) * 16
    coupling = coupling_matrix(triple_out, triple_in, triple_coef, triple_value, modes, coefs)
    devices = lax.axis_size("tile")
    up = [(i, i + 1) for i in range(devices - 1)]
    down = [(j, i) for i, j in up]

    def extend(shard):
        before = lax.ppermute(shard[:, -1:], "tile", up)
        after = lax.ppermute(shard[:, :1], "tile", down)
        return [jnp.transpose(part, (1, 2, 0, 3)) for part in (shard, before, after)]

    m_parts = extend(mode_field)
    k_parts = extend(conductivity)
    vmem = pl.BlockSpec(memory_space=pltpu.VMEM)
    out = pl.pallas_call(
        functools.partial(main_kernel, coefs, modes, depth, rows),
        out_shape=jax.ShapeDtypeStruct((depth, rows, modes, lanes), jnp.bfloat16),
        in_specs=[vmem] * 7,
        out_specs=vmem,
        scratch_shapes=[
            pltpu.VMEM((depth + 2, rows + 2, LANES, lanes), jnp.bfloat16),
            pltpu.VMEM((depth + 2, rows + 2, coefs_pad, lanes), jnp.bfloat16),
            pltpu.VMEM((2, 6, LANES, LANES), jnp.bfloat16),
            pltpu.VMEM((2, 6, coefs_pad, LANES), jnp.float32),
            pltpu.VMEM((2, 6, coefs, 16, LANES), jnp.bfloat16),
            pltpu.VMEM((1, coefs * LANES, 2 * LANES), jnp.bfloat16),
        ],
        compiler_params=pltpu.CompilerParams(vmem_limit_bytes=48 << 20),
    )(coupling, *m_parts, *k_parts)
    return jnp.transpose(out, (2, 0, 1, 3))


def solution(mesh):
    return jax.shard_map(
        per_device,
        mesh=mesh,
        in_specs=(
            P(None, ("rep", "tile"), None, None),
            P(None, ("rep", "tile"), None, None),
            P(),
            P(),
            P(),
            P(),
        ),
        out_specs=P(None, ("rep", "tile"), None, None),
        check_vma=False,
    )
```
